32 devices in a mesh: dp: 8 (over y, x, core), mp: 4 (over z).
Axes of the slice: x: 2, y: 2, z: 4, core: 2. Of those that a mesh axis runs over, the one named last changes fastest.
Arguments:
- fields: bfloat16 [8, 128, 20, 128, 128], P('dp', 'mp'), may hold values from -6 to 6
- cotangent: bfloat16 [8, 128, 20, 128, 128], P('dp', 'mp'), may hold values from -3 to 3
- spectral_weight: bfloat16 [32, 2, 20, 20, 512], P('dp', None, None, None, 'mp'), may hold values from -5 to 5
- conv_weight: bfloat16 [20, 20], replicated, may hold values from -1.25 to 1.25
- conv_bias: float32 [20], replicated, may hold values from -3 to 3
Outputs:
- spectral_grad: float32 [32, 2, 20, 20, 512], P('dp', None, None, None, 'mp')
The draws below stay inside these ranges and needn't reach their ends.
All inputs are finite; a program needn't handle non-finite values.
Results may differ from the reference program's by a relative error of at most 0.0085.
Values may be sent and summed in bfloat16 or wider, within the bound.
A program may use at most 320 MiB of HBM per device.

```python
import math
import jax
import jax.numpy as jnp
from jax import lax

X = 128
Y = 128
Z = 128
C = 20
KX = 32
KY = 32
KZ = 16
SAMPLES = 8


def block_levels(own_key, shape, shards, least, top_value):
    def one(position, shards_of):
        steps = jax.random.uniform(jax.random.fold_in(jax.random.fold_in(own_key, 6), position), (shards_of,), jnp.float32, least / len(shards), top_value / len(shards))
        return jnp.repeat(jnp.exp(steps), shape[position] // shards_of).reshape((-1,) + (1,) * (len(shape) - position - 1))

    gain = one(*shards[0])
    for cut in shards[1:]:
        gain = gain * one(*cut)
    return gain


def centred(key, extent, spread, most, shards=(), held_as=jnp.bfloat16):
    gain = block_levels(key, extent, shards, -0.22, 0.18) if shards else 1.0
    drawn = jax.random.normal(key, extent, jnp.float32) * spread * gain
    return jnp.minimum(jnp.maximum(drawn, -most), most).astype(held_as)


def setup_inputs(seed: int = 0) -> dict:
    splits = jax.random.split(jax.random.key(seed), 6)
    fields = centred(splits[0], (SAMPLES, X, C, Y, Z), 1.0, 6.0, ((0, 8), (1, 4)))
    cotangent = centred(splits[1], (SAMPLES, X, C, Y, Z), 0.5, 3.0, ((0, 8), (1, 4)))
    spectral_weight = centred(splits[2], (KX, 2, C, C, KY * KZ), 1.0, 5.0, ((0, 8), (4, 4)))
    conv_weight = centred(splits[3], (C, C), C ** -0.5, 1.25)
    conv_bias = centred(splits[4], (C,), 0.5, 3.0, (), jnp.float32)
    return dict(fields=fields, cotangent=cotangent, spectral_weight=spectral_weight, conv_weight=conv_weight, conv_bias=conv_bias)


inv_root_two = 0.7071067811865476
inv_root_two_pi = 0.3989422804014327


def kept_modes(count, length):
    indices = jnp.arange(count, dtype=jnp.int32)
    return jnp.where(indices < count // 2, indices, length - count + indices).astype(jnp.int32)


def gelu_slope(values):
    return 0.5 * (1.0 + lax.erf(values * inv_root_two)) + values * jnp.exp(-0.5 * values * values) * inv_root_two_pi


def reference(fields, cotangent, spectral_weight, conv_weight, conv_bias):
    highest = lax.Precision.HIGHEST
    rows_x = kept_modes(KX, X)
    rows_y = kept_modes(KY, Y)
    modes_z = jnp.arange(KZ, dtype=jnp.int32)
    cells_z = jnp.arange(Z, dtype=jnp.int32)
    phases = (2.0 * math.pi / Z) * ((modes_z[:, None] * cells_z[None, :]) % Z).astype(jnp.float32)
    weight_z = jnp.where(modes_z == 0, 1.0, 2.0).astype(jnp.float32)
    cos_z = weight_z[:, None] * jnp.cos(phases) / Z
    sin_z = weight_z[:, None] * jnp.sin(phases) / Z
    scale_back = weight_z / (X * Y * Z)
    weights = spectral_weight.astype(jnp.float32).reshape(KX, 2, C, C, KY, KZ)
    real_w = weights[:, 0]
    imag_w = weights[:, 1]
    mixing = conv_weight.astype(jnp.float32)

    def truncate(volume):
        full_spec = jnp.fft.rfftn(volume, axes=(0, 2, 3))
        kept_spec = full_spec[rows_x][:, :, rows_y][..., :KZ]
        return jnp.real(kept_spec).astype(jnp.float32), jnp.imag(kept_spec).astype(jnp.float32)

    def place(values):
        section = jnp.zeros((X, C, KY, KZ), jnp.float32).at[rows_x].set(values)
        return jnp.zeros((X, C, Y, KZ), jnp.float32).at[:, :, rows_y].set(section)

    def one_sample(total, inputs):
        sample, cot_sample = inputs
        volume = sample.astype(jnp.float32)
        spec_re, spec_im = truncate(volume)
        mixed_re = jnp.einsum('acbd,acobd->aobd', spec_re, real_w, precision=highest) - jnp.einsum('acbd,acobd->aobd', spec_im, imag_w, precision=highest)
        mixed_im = jnp.einsum('acbd,acobd->aobd', spec_re, imag_w, precision=highest) + jnp.einsum('acbd,acobd->aobd', spec_im, real_w, precision=highest)
        spectrum = place(mixed_re) + 1j * place(mixed_im)
        inverse_xy = jnp.fft.ifft2(spectrum, axes=(0, 2))
        spectral = jnp.einsum('xoyk,kz->xoyz', jnp.real(inverse_xy).astype(jnp.float32), cos_z, precision=highest) - jnp.einsum('xoyk,kz->xoyz', jnp.imag(inverse_xy).astype(jnp.float32), sin_z, precision=highest)
        conv_term = jnp.einsum('xcyz,co->xoyz', volume, mixing, precision=highest)
        pre_act = spectral + conv_term + conv_bias[None, :, None, None]
        grad_pre = (cot_sample.astype(jnp.float32) * gelu_slope(pre_act)).astype(jnp.bfloat16)
        back_re, back_im = truncate(grad_pre.astype(jnp.float32))
        back_re = back_re * scale_back
        back_im = back_im * scale_back
        grad_re = jnp.einsum('acbd,aobd->acobd', spec_re, back_re, precision=highest) + jnp.einsum('acbd,aobd->acobd', spec_im, back_im, precision=highest)
        grad_im = jnp.einsum('acbd,aobd->acobd', spec_re, back_im, precision=highest) - jnp.einsum('acbd,aobd->acobd', spec_im, back_re, precision=highest)
        term = jnp.stack([grad_re, grad_im], axis=1).reshape(KX, 2, C, C, KY * KZ)
        return total + term, None

    start_total = jnp.zeros((KX, 2, C, C, KY * KZ), jnp.float32)
    result, unused = lax.scan(one_sample, start_total, (fields, cotangent))
    return result
```

```python
import functools
import math

import jax
import jax.numpy as jnp
import ml_dtypes
import numpy as np
from jax import lax
from jax.experimental import pallas as pl
from jax.experimental.pallas import tpu as pltpu
from jax.sharding import PartitionSpec as P

KX = 32
KY = 32
KZ = 16
ROWS = 16
VMEM_BYTES = 50 * 2**20

f32 = jnp.float32
bf16 = jnp.bfloat16


def kept_modes(count, length):
    indices = np.arange(count)
    return np.where(indices < count // 2, indices, length - count + indices)


def rounded(values):
    return np.asarray(values, np.float32).astype(ml_dtypes.bfloat16)


def split_parts(values):
    upper = rounded(values)
    return upper, rounded(values - upper.astype(np.float64))


def make_tables(x_cells, y_cells, z_cells, slabs):
    slab_len = x_cells // slabs
    kx = kept_modes(KX, x_cells)
    kx = np.where(kx >= x_cells // 2, kx - x_cells, kx)
    part = np.exp(-2j * math.pi * np.outer(kx, np.arange(slab_len)) / x_cells)
    left, scale, right = np.linalg.svd(part, full_matrices=False)
    rank = int(np.sum(scale > scale[0] * np.finfo(np.float32).eps))
    rank = min(rank + rank % 2, slab_len)
    left = left[:, :rank] * scale[:rank]
    right = right[:rank]
    shifts = np.exp(-2j * math.pi * np.outer(kx, np.arange(slabs) * slab_len) / x_cells)
    outer = shifts[:, :, None] * left[:, None, :]
    table_x = np.zeros((KX, 2, slabs, rank, 2))
    table_x[:, 0, :, :, 0] = outer.real
    table_x[:, 0, :, :, 1] = -outer.imag
    table_x[:, 1, :, :, 0] = outer.imag
    table_x[:, 1, :, :, 1] = outer.real
    table_x = table_x.reshape(KX * 2, slabs * rank * 2)
    wave_z = np.exp(-2j * math.pi * np.outer(np.arange(z_cells), np.arange(KZ)) / z_cells)
    inner = right.T[:, None, :, None] * wave_z[None, :, None, :]
    table_zx = np.zeros((slab_len, 2, z_cells, rank, 2, KZ))
    table_zx[:, 0, :, :, 0] = inner.real
    table_zx[:, 1, :, :, 0] = -inner.imag
    table_zx[:, 0, :, :, 1] = inner.imag
    table_zx[:, 1, :, :, 1] = inner.real
    table_zx = table_zx.reshape(slab_len, 2 * z_cells, rank * 2 * KZ)
    phase_y = 2.0 * math.pi * np.outer(kept_modes(KY, y_cells), np.arange(y_cells)) / y_cells
    table_y = np.concatenate([np.cos(phase_y), -np.sin(phase_y)], axis=0)
    return rank, table_x, table_zx, table_y


def dot(left, right, contract=((1,), (0,))):
    return lax.dot_general(left, right, (contract, ((), ())), preferred_element_type=f32)


def y_modes(pair, table, modes_ref, channel, z_cells):
    both = dot(table, pair)
    half = 2 * KY
    total = both[:half] + both[half:]
    for i in range(2):
        one = total[:, i * z_cells : (i + 1) * z_cells].astype(bf16)
        rows = pl.ds((channel + i) * KY, KY)
        modes_ref[rows, :z_cells] = one[:KY]
        modes_ref[rows, z_cells:] = one[KY:]


def forward_kernel(fields_ref, table_y_ref, table_zx_ref, out_ref, modes_ref, total_ref):
    channels, _, z_cells = fields_ref.shape[1:]
    step = pl.program_id(0)
    table = table_y_ref[...]
    for c in range(0, channels, 2):
        pair = jnp.concatenate([fields_ref[0, c], fields_ref[0, c + 1]], axis=1)
        y_modes(pair, table, modes_ref, c, z_cells)
    term = dot(modes_ref[...], table_zx_ref[0])

    @pl.when(step == 0)
    def _():
        total_ref[...] = term

    @pl.when(step > 0)
    def _():
        total_ref[...] += term

    @pl.when(step == pl.num_programs(0) - 1)
    def _():
        out_ref[...] = total_ref[...].astype(bf16)


def gelu_slope(values):
    size = jnp.abs(values)
    bell = jnp.exp(values * values * -0.5)
    base = 1.0 + size * (0.3275911 * math.sqrt(0.5))
    t = pl.reciprocal(base, approx=True)
    t = t * (2.0 - base * t)
    tail = t * (
        0.5 * 0.254829592
        + t * (0.5 * -0.284496736 + t * (0.5 * 1.421413741 + t * (0.5 * -1.453152027 + t * (0.5 * 1.061405429))))
    )
    part = bell * (size * 0.3989422804014327 - tail)
    return jnp.where(values >= 0.0, 1.0 + part, -part)


def slope_kernel(
    bias_ref,
    fields_ref,
    cotangent_ref,
    mixed_ref,
    conv_ref,
    table_y_ref,
    inverse_y_ref,
    table_zx_ref,
    out_ref,
    back_ref,
    pre_ref,
    modes_ref,
    total_ref,
):
    channels, y_cells, z_cells = fields_ref.shape[1:]
    step = pl.program_id(0)
    table = table_y_ref[...]
    inverse_y = inverse_y_ref[...]
    mixing = conv_ref[...]
    back_ref[...] = dot(mixed_ref[...], table_zx_ref[0], ((1,), (1,))).astype(bf16)
    for g in range(0, y_cells, 2 * ROWS):
        pair = jnp.concatenate(
            [
                fields_ref[0, :, g : g + ROWS, :].reshape(channels * ROWS, z_cells),
                fields_ref[0, :, g + ROWS : g + 2 * ROWS, :].reshape(channels * ROWS, z_cells),
            ],
            axis=1,
        )
        conv = dot(mixing, pair)
        pre_ref[:, g : g + ROWS, :] = conv[:, :z_cells].reshape(channels, ROWS, z_cells)
        pre_ref[:, g + ROWS : g + 2 * ROWS, :] = conv[:, z_cells:].reshape(channels, ROWS, z_cells)
    for o in range(0, channels, 2):
        columns = []
        for i in range(2):
            one = back_ref[(o + i) * KY : (o + i + 1) * KY, :]
            columns.append(jnp.concatenate([one[:, :z_cells], one[:, z_cells:]], axis=0))
        spectral = dot(inverse_y, jnp.concatenate(columns, axis=1))
        deltas = []
        for i in range(2):
            pre = spectral[:, i * z_cells : (i + 1) * z_cells] + pre_ref[o + i] + bias_ref[o + i]
            deltas.append((cotangent_ref[0, o + i].astype(f32) * gelu_slope(pre)).astype(bf16))
        y_modes(jnp.concatenate(deltas, axis=1), table, modes_ref, o, z_cells)
    term = dot(modes_ref[...], table_zx_ref[0])

    @pl.when(step == 0)
    def _():
        total_ref[...] = term

    @pl.when(step > 0)
    def _():
        total_ref[...] += term

    @pl.when(step == pl.num_programs(0) - 1)
    def _():
        out_ref[...] = total_ref[...].astype(bf16)


def mix_kernel(spectra_ref, weight_ref, scale_ref, out_ref):
    samples, _, _, channels, _ = spectra_ref.shape
    scale = scale_ref[...]

    def one_sample(s, carry):
        real = jnp.zeros(out_ref.shape[3:], f32)
        imag = jnp.zeros(out_ref.shape[3:], f32)
        spec_re = spectra_ref[s, 0, 0].astype(f32) * scale
        spec_im = spectra_ref[s, 0, 1].astype(f32) * scale
        for c in range(channels):
            real_w = weight_ref[0, 0, c].astype(f32)
            imag_w = weight_ref[0, 1, c].astype(f32)
            real += spec_re[c : c + 1] * real_w - spec_im[c : c + 1] * imag_w
            imag += spec_re[c : c + 1] * imag_w + spec_im[c : c + 1] * real_w
        out_ref[s, 0, 0] = real.astype(out_ref.dtype)
        out_ref[s, 0, 1] = imag.astype(out_ref.dtype)
        return carry

    lax.fori_loop(0, samples, one_sample, 0)


def grad_kernel(spectra_ref, back_ref, scale_ref, out_ref):
    samples, _, _, channels, _ = spectra_ref.shape
    scale = scale_ref[...]
    for c in range(channels):
        real = jnp.zeros(out_ref.shape[3:], f32)
        imag = jnp.zeros(out_ref.shape[3:], f32)
        for s in range(samples):
            spec_re = spectra_ref[s, 0, 0, c : c + 1].astype(f32)
            spec_im = spectra_ref[s, 0, 1, c : c + 1].astype(f32)
            back_re = back_ref[s, 0, 0].astype(f32)
            back_im = back_ref[s, 0, 1].astype(f32)
            real += spec_re * back_re + spec_im * back_im
            imag += spec_re * back_im - spec_im * back_re
        out_ref[0, 0, c] = real * scale
        out_ref[0, 1, c] = imag * scale


def shards(fields, cotangent, spectral_weight, conv_weight, conv_bias):
    _, slab_len, channels, y_cells, z_cells = fields.shape
    slabs = lax.axis_size("mp")
    data_count = lax.axis_size("dp")
    kx_local = spectral_weight.shape[0]
    ky_local = KY // slabs
    x_cells = slab_len * slabs
    rank, table_x, table_zx, table_y = make_tables(x_cells, y_cells, z_cells, slabs)
    lanes = rank * 2 * KZ
    table_x = jnp.asarray(table_x.astype(np.float32))
    table_zx = jnp.asarray(rounded(table_zx))
    y_parts = jnp.asarray(np.concatenate(split_parts(table_y), axis=0))
    inverse_y = jnp.asarray(rounded(table_y.T))
    weight_z = np.where(np.arange(KZ) == 0, 1.0, 2.0) / (x_cells * y_cells * z_cells)
    scale = jnp.asarray(np.tile(weight_z, ky_local)[None].astype(np.float32))
    mixing = jnp.kron(conv_weight.T, jnp.eye(ROWS, dtype=bf16))
    mode_cells = ky_local * KZ

    cell_spec = pl.BlockSpec((1, channels, y_cells, z_cells), lambda x: (x, 0, 0, 0))
    zx_spec = pl.BlockSpec((1, 2 * z_cells, lanes), lambda x: (x, 0, 0))

    def whole(shape):
        return pl.BlockSpec(shape, lambda x: (0,) * len(shape))

    params = pltpu.CompilerParams(
        dimension_semantics=("arbitrary",), vmem_limit_bytes=VMEM_BYTES
    )
    coefs_shape = (channels * KY, lanes)
    coefs_out = jax.ShapeDtypeStruct(coefs_shape, bf16)
    work = [
        pltpu.VMEM((channels * KY, 2 * z_cells), bf16),
        pltpu.VMEM(coefs_shape, f32),
    ]

    def to_modes(coefs):
        packed = coefs.reshape(channels, slabs, ky_local, rank * 2, KZ)
        packed = jnp.transpose(packed, (1, 3, 0, 2, 4)).reshape(slabs, rank * 2, -1)
        moved = lax.all_to_all(packed, "mp", split_axis=0, concat_axis=0, tiled=True)
        moved = moved.reshape(slabs * rank * 2, -1).astype(f32)
        return jnp.dot(table_x, moved, precision=lax.Precision.HIGHEST)

    def across_samples(modes):
        modes = modes.reshape(data_count, kx_local * 2, -1)
        moved = lax.all_to_all(modes, "dp", split_axis=0, concat_axis=0, tiled=True)
        return moved.reshape(data_count, kx_local, 2, channels, mode_cells)

    with jax.named_scope("forward_fields"):
        coefs = pl.pallas_call(
            forward_kernel,
            grid=(slab_len,),
            in_specs=[cell_spec, whole(y_parts.shape), zx_spec],
            out_specs=whole(coefs_shape),
            out_shape=coefs_out,
            scratch_shapes=work,
            compiler_params=params,
        )(fields[0], y_parts, table_zx)
    sample_spectra = across_samples(to_modes(coefs))

    sample_spec = pl.BlockSpec(
        (data_count, 1, 2, channels, mode_cells), lambda k: (0, k, 0, 0, 0)
    )
    weight_spec = pl.BlockSpec(
        (1, 2, channels, channels, mode_cells), lambda k: (k, 0, 0, 0, 0)
    )
    with jax.named_scope("mix_modes"):
        local_mixed = pl.pallas_call(
            mix_kernel,
            grid=(kx_local,),
            in_specs=[sample_spec, weight_spec, whole(scale.shape)],
            out_specs=sample_spec,
            out_shape=jax.ShapeDtypeStruct(sample_spectra.shape, bf16),
            compiler_params=params,
        )(sample_spectra, spectral_weight, scale)
    returned = lax.all_to_all(
        local_mixed.reshape(data_count, kx_local * 2, -1),
        "dp",
        split_axis=0,
        concat_axis=0,
        tiled=True,
    )
    mixed = returned.reshape(KX * 2, -1).astype(f32)
    slab_mixed = jnp.dot(table_x.T, mixed, precision=lax.Precision.HIGHEST).astype(bf16)
    moved = lax.all_to_all(
        slab_mixed.reshape(slabs, rank * 2, -1), "mp", split_axis=0, concat_axis=0, tiled=True
    )
    moved = moved.reshape(slabs, rank * 2, channels, ky_local, KZ)
    mixed_coefs = jnp.transpose(moved, (2, 0, 3, 1, 4)).reshape(coefs_shape)

    with jax.named_scope("slope_and_back"):
        back_coefs = pl.pallas_call(
            slope_kernel,
            grid=(slab_len,),
            in_specs=[
                pl.BlockSpec(memory_space=pltpu.SMEM),
                cell_spec,
                cell_spec,
                whole(coefs_shape),
                whole(mixing.shape),
                whole(y_parts.shape),
                whole(inverse_y.shape),
                zx_spec,
            ],
            out_specs=whole(coefs_shape),
            out_shape=coefs_out,
            scratch_shapes=[
                pltpu.VMEM((channels * KY, 2 * z_cells), bf16),
                pltpu.VMEM((channels, y_cells, z_cells), f32),
            ]
            + work,
            compiler_params=params,
        )(conv_bias, fields[0], cotangent[0], mixed_coefs, mixing, y_parts, inverse_y, table_zx)
    sample_back = across_samples(to_modes(back_coefs))

    with jax.named_scope("weight_gradient"):
        return pl.pallas_call(
            grad_kernel,
            grid=(kx_local,),
            in_specs=[sample_spec, sample_spec, whole(scale.shape)],
            out_specs=weight_spec,
            out_shape=jax.ShapeDtypeStruct(spectral_weight.shape, f32),
            compiler_params=params,
        )(sample_spectra, sample_back, scale)


def solution(mesh):
    return jax.shard_map(
        shards,
        mesh=mesh,
        in_specs=(
            P("dp", "mp", None, None, None),
            P("dp", "mp", None, None, None),
            P("dp", None, None, None, "mp"),
            P(),
            P(),
        ),
        out_specs=P("dp", None, None, None, "mp"),
        check_vma=False,
    )
```

```python
import functools
import math

import jax
import jax.numpy as jnp
import ml_dtypes
import numpy as np
from jax import lax
from jax.experimental import pallas as pl
from jax.experimental.pallas import tpu as pltpu
from jax.sharding import PartitionSpec as P

KX = 32
KY = 32
KZ = 16
ROWS = 16
VMEM_BYTES = 50 * 2**20

f32 = jnp.float32
bf16 = jnp.bfloat16


def kept_modes(count, length):
    indices = np.arange(count)
    return np.where(indices < count // 2, indices, length - count + indices)


def rounded(values):
    return np.asarray(values, np.float32).astype(ml_dtypes.bfloat16)


def split_parts(values):
    upper = rounded(values)
    return upper, rounded(values - upper.astype(np.float64))


def make_tables(x_cells, y_cells, z_cells, slabs):
    slab_len = x_cells // slabs
    kx = kept_modes(KX, x_cells)
    kx = np.where(kx >= x_cells // 2, kx - x_cells, kx)
    part = np.exp(-2j * math.pi * np.outer(kx, np.arange(slab_len)) / x_cells)
    left, scale, right = np.linalg.svd(part, full_matrices=False)
    rank = int(np.sum(scale > scale[0] * np.finfo(np.float32).eps))
    rank = min(rank + rank % 2, slab_len)
    left = left[:, :rank] * scale[:rank]
    right = right[:rank]
    shifts = np.exp(-2j * math.pi * np.outer(kx, np.arange(slabs) * slab_len) / x_cells)
    outer = shifts[:, :, None] * left[:, None, :]
    table_x = np.zeros((KX, 2, slabs, rank, 2))
    table_x[:, 0, :, :, 0] = outer.real
    table_x[:, 0, :, :, 1] = -outer.imag
    table_x[:, 1, :, :, 0] = outer.imag
    table_x[:, 1, :, :, 1] = outer.real
    table_x = table_x.reshape(KX * 2, slabs, rank * 2)
    table_x = np.stack([np.kron(table_x[:, m].T, np.eye(KZ)) for m in range(slabs)])
    wave_z = np.exp(-2j * math.pi * np.outer(np.arange(z_cells), np.arange(KZ)) / z_cells)
    inner = right.T[:, None, :, None] * wave_z[None, :, None, :]
    table_zx = np.zeros((slab_len, 2, z_cells, rank, 2, KZ))
    table_zx[:, 0, :, :, 0] = inner.real
    table_zx[:, 1, :, :, 0] = -inner.imag
    table_zx[:, 0, :, :, 1] = inner.imag
    table_zx[:, 1, :, :, 1] = inner.real
    table_zx = table_zx.reshape(slab_len, 2 * z_cells, rank * 2 * KZ)
    phase_y = 2.0 * math.pi * np.outer(kept_modes(KY, y_cells), np.arange(y_cells)) / y_cells
    table_y = np.concatenate([np.cos(phase_y), -np.sin(phase_y)], axis=0)
    return rank, table_x, table_zx, table_y


def dot(left, right, contract=((1,), (0,))):
    return lax.dot_general(left, right, (contract, ((), ())), preferred_element_type=f32)


def y_modes(pair, table, modes_ref, channel, z_cells, offset=0):
    both = dot(table, pair)
    half = 2 * KY
    total = both[:half] + both[half:]
    for i in range(2):
        one = total[:, i * z_cells : (i + 1) * z_cells].astype(bf16)
        rows = pl.ds((channel + i) * KY, KY)
        modes_ref[rows, offset : offset + z_cells] = one[:KY]
        modes_ref[rows, offset + z_cells : offset + 2 * z_cells] = one[KY:]


def column_chunks(lanes):
    return [(start, min(start + 256, lanes)) for start in range(0, lanes, 256)]


def store_blocks(total_ref, out_ref, channels):
    blocks, rows, _ = out_ref.shape
    ky_local = rows // channels
    group = max(1, ROWS // ky_local)
    for b in range(blocks):
        for c in range(0, channels, group):
            parts = [
                total_ref[(c + i) * KY + b * ky_local : (c + i) * KY + (b + 1) * ky_local, :]
                for i in range(group)
            ]
            out_ref[b, c * ky_local : (c + group) * ky_local, :] = jnp.concatenate(
                parts, axis=0
            ).astype(bf16)


def forward_kernel(fields_ref, table_y_ref, table_zx_ref, out_ref, first_ref, second_ref, total_ref):
    cells, channels, _, z_cells = fields_ref.shape
    lanes = total_ref.shape[1]
    step = pl.program_id(0)
    table = table_y_ref[...]

    @pl.when(step == 0)
    def _():
        total_ref[...] = jnp.zeros_like(total_ref)

    def inner(modes_ref, cell, start, stop):
        both = table_zx_ref[cell : cell + 2, :, start:stop].reshape(4 * z_cells, stop - start)
        total_ref[:, start:stop] += dot(modes_ref[...], both)

    pending = []
    for half, modes_ref in enumerate((first_ref, second_ref)):
        cell = 2 * half
        for c in range(0, channels, 2):
            for i in range(2):
                pair = jnp.concatenate(
                    [fields_ref[cell + i, c], fields_ref[cell + i, c + 1]], axis=1
                )
                y_modes(pair, table, modes_ref, c, z_cells, 2 * i * z_cells)
            if pending and c % 4 == 2:
                pending.pop(0)()
        for todo in pending:
            todo()
        pending = [
            functools.partial(inner, modes_ref, cell, start, stop)
            for start, stop in column_chunks(lanes)
        ]
    for todo in pending:
        todo()

    @pl.when(step == pl.num_programs(0) - 1)
    def _():
        store_blocks(total_ref, out_ref, channels)


def gelu_slope(values):
    size = jnp.abs(values)
    bell = jnp.exp2(values * values * (-0.5 * math.log2(math.e)))
    t = pl.reciprocal(1.0 + size * (0.3275911 * math.sqrt(0.5)), approx=True)
    tail = t * (
        0.5 * 0.254829592
        + t * (0.5 * -0.284496736 + t * (0.5 * 1.421413741 + t * (0.5 * -1.453152027 + t * (0.5 * 1.061405429))))
    )
    part = bell * (size * 0.3989422804014327 - tail)
    return jnp.where(values >= 0.0, 1.0 + part, -part)


def slope_kernel(
    bias_ref,
    fields_first_ref,
    fields_odd_ref,
    fields_next_ref,
    cotangent_ref,
    mixed_ref,
    conv_ref,
    table_y_ref,
    inverse_y_ref,
    zx_before_ref,
    zx_even_ref,
    zx_odd_ref,
    zx_next_ref,
    out_ref,
    rows_ref,
    back_even_ref,
    back_odd_ref,
    pre_even_ref,
    pre_odd_ref,
    modes_even_ref,
    modes_odd_ref,
    total_ref,
):
    _, channels, y_cells, z_cells = cotangent_ref.shape
    lanes = total_ref.shape[1]
    count = channels * KY
    step = pl.program_id(0)
    last = pl.num_programs(0) - 1
    table = table_y_ref[...]
    inverse_y = inverse_y_ref[...]
    mixing = conv_ref[...]

    def ahead(fields_ref, zx_ref, back_ref, pre_ref):
        def inverse(start, stop):
            back_ref[start:stop, :] = dot(
                rows_ref[start:stop, :], zx_ref[0], ((1,), (1,))
            ).astype(bf16)

        def convolve(g):
            pair = jnp.concatenate(
                [
                    fields_ref[0, :, g : g + ROWS, :].reshape(channels * ROWS, z_cells),
                    fields_ref[0, :, g + ROWS : g + 2 * ROWS, :].reshape(channels * ROWS, z_cells),
                ],
                axis=1,
            )
            conv = dot(mixing, pair)
            for i in range(2):
                rows = slice(g + i * ROWS, g + (i + 1) * ROWS)
                pre_ref[:, rows, :] = conv[:, i * z_cells : (i + 1) * z_cells].reshape(
                    channels, ROWS, z_cells
                )

        return [
            functools.partial(inverse, 0, count // 2),
            functools.partial(inverse, count // 2, count),
        ] + [functools.partial(convolve, g) for g in range(0, y_cells, 2 * ROWS)]

    def behind(modes_ref, zx_ref):
        def inner(start, stop):
            total_ref[:, start:stop] += dot(modes_ref[...], zx_ref[0, :, start:stop])

        return [functools.partial(inner, start, stop) for start, stop in column_chunks(lanes)]

    def here(cell, back_ref, pre_ref, modes_ref, o):
        columns = []
        for i in range(2):
            one = back_ref[(o + i) * KY : (o + i + 1) * KY, :]
            columns.append(jnp.concatenate([one[:, :z_cells], one[:, z_cells:]], axis=0))
        spectral = dot(inverse_y, jnp.concatenate(columns, axis=1))
        deltas = []
        for i in range(2):
            pre = spectral[:, i * z_cells : (i + 1) * z_cells] + pre_ref[o + i] + bias_ref[o + i]
            deltas.append((cotangent_ref[cell, o + i].astype(f32) * gelu_slope(pre)).astype(bf16))
        y_modes(jnp.concatenate(deltas, axis=1), table, modes_ref, o, z_cells)

    @pl.when(step == 0)
    def _():
        blocks = mixed_ref.shape[0]
        per_block = mixed_ref.shape[1]
        ky_local = per_block // channels
        for b in range(blocks):
            total_ref[b * per_block : (b + 1) * per_block, :] = mixed_ref[b].astype(f32)
        for o in range(channels):
            parts = [
                total_ref[b * per_block + o * ky_local : b * per_block + (o + 1) * ky_local, :]
                for b in range(blocks)
            ]
            rows_ref[o * KY : (o + 1) * KY, :] = jnp.concatenate(parts, axis=0).astype(bf16)
        total_ref[...] = jnp.zeros_like(total_ref)
        modes_odd_ref[...] = jnp.zeros_like(modes_odd_ref)
        for todo in ahead(fields_first_ref, zx_even_ref, back_even_ref, pre_even_ref):
            todo()

    even = (back_even_ref, pre_even_ref, modes_even_ref)
    odd = (back_odd_ref, pre_odd_ref, modes_odd_ref)
    for cell, own, beside in (
        (
            0,
            even,
            behind(modes_odd_ref, zx_before_ref)
            + ahead(fields_odd_ref, zx_odd_ref, back_odd_ref, pre_odd_ref),
        ),
        (
            1,
            odd,
            behind(modes_even_ref, zx_even_ref)
            + ahead(fields_next_ref, zx_next_ref, back_even_ref, pre_even_ref),
        ),
    ):
        for o in range(0, channels, 2):
            if beside:
                beside.pop(0)()
            here(cell, *own, o)
        for todo in beside:
            todo()

    @pl.when(step == last)
    def _():
        for todo in behind(modes_odd_ref, zx_odd_ref):
            todo()
        store_blocks(total_ref, out_ref, channels)


def to_modes_kernel(coefs_ref, upper_ref, lower_ref, out_ref):
    total = jnp.zeros((coefs_ref.shape[1], upper_ref.shape[2]), f32)
    for m in range(coefs_ref.shape[0]):
        total += dot(coefs_ref[m], upper_ref[m]) + dot(coefs_ref[m], lower_ref[m])
    width = out_ref.shape[2]
    for i in range(out_ref.shape[0]):
        out_ref[i] = total[:, i * width : (i + 1) * width]


def from_modes_kernel(modes_ref, upper_ref, lower_ref, out_ref):
    modes = jnp.concatenate([modes_ref[i] for i in range(modes_ref.shape[0])], axis=1)
    flip = ((1,), (1,))
    out_ref[0] = (dot(modes, upper_ref[0], flip) + dot(modes, lower_ref[0], flip)).astype(bf16)


def swap_groups(parts):
    lanes = parts[0].shape[1]
    group = lax.broadcasted_iota(jnp.int32, parts[0].shape, 1) // KZ
    results = []
    for j in range(len(parts)):
        total = parts[j]
        for i, part in enumerate(parts):
            if i != j:
                moved = pltpu.roll(part, ((i - j) * KZ) % lanes, 1)
                total = jnp.where(group == i, moved, total)
        results.append(total)
    return results


def open_rows(wire_ref, s, channels):
    ky_local = wire_ref.shape[1] // channels
    return swap_groups(
        [wire_ref[s, pl.ds(k, channels, stride=ky_local), :] for k in range(ky_local)]
    )


def mix_kernel(blocked, spectra_ref, weight_ref, scale_ref, out_ref, opened_ref, rows_ref):
    samples = spectra_ref.shape[0]
    kx_local, _, channels, _, mode_cells = weight_ref.shape
    scale = scale_ref[...]

    def one_sample(s, carry):
        if blocked:
            for g, part in enumerate(open_rows(spectra_ref, s, channels)):
                opened_ref[s, g] = part
        else:
            opened_ref[s] = spectra_ref[s]
        results = []
        for k in range(kx_local):
            real = jnp.zeros((channels, mode_cells), f32)
            imag = jnp.zeros((channels, mode_cells), f32)
            for c in range(channels):
                spec_re = opened_ref[s, 2 * k, c : c + 1, :]
                spec_im = opened_ref[s, 2 * k + 1, c : c + 1, :]
                real_w = weight_ref[k, 0, c].astype(f32)
                imag_w = weight_ref[k, 1, c].astype(f32)
                real += spec_re * real_w - spec_im * imag_w
                imag += spec_re * imag_w + spec_im * real_w
            results += [real * scale, imag * scale]
        if blocked:
            ky_local = rows_ref.shape[0] // channels
            for k, part in enumerate(swap_groups(results)):
                rows_ref[pl.ds(k, channels, stride=ky_local), :] = part
            out_ref[s] = rows_ref[...].astype(bf16)
        else:
            for g, part in enumerate(results):
                out_ref[s, g] = part.astype(bf16)
        return carry

    lax.fori_loop(0, samples, one_sample, 0)


def grad_kernel(blocked, spectra_ref, back_ref, scale_ref, out_ref, opened_ref):
    kx_local, _, channels, _, mode_cells = out_ref.shape
    samples = spectra_ref.shape[0]
    scale = scale_ref[...]
    for s in range(samples):
        if blocked:
            for g, part in enumerate(open_rows(back_ref, s, channels)):
                opened_ref[s, g] = part * scale
        else:
            opened_ref[s] = back_ref[s] * scale

    def one_channel(c, carry):
        for k in range(kx_local):
            real = jnp.zeros((channels, mode_cells), f32)
            imag = jnp.zeros((channels, mode_cells), f32)
            for s in range(samples):
                spec_re = spectra_ref[s, 2 * k, pl.ds(c, 1), :]
                spec_im = spectra_ref[s, 2 * k + 1, pl.ds(c, 1), :]
                back_re = opened_ref[s, 2 * k]
                back_im = opened_ref[s, 2 * k + 1]
                real += spec_re * back_re + spec_im * back_im
                imag += spec_re * back_im - spec_im * back_re
            out_ref[k, 0, c] = real
            out_ref[k, 1, c] = imag
        return carry

    lax.fori_loop(0, channels, one_channel, 0)


def shards(fields, cotangent, spectral_weight, conv_weight, conv_bias):
    _, slab_len, channels, y_cells, z_cells = fields.shape
    slabs = lax.axis_size("mp")
    data_count = lax.axis_size("dp")
    kx_local = spectral_weight.shape[0]
    ky_local = KY // slabs
    x_cells = slab_len * slabs
    rank, table_x, table_zx, table_y = make_tables(x_cells, y_cells, z_cells, slabs)
    lanes = rank * 2 * KZ
    x_upper, x_lower = (jnp.asarray(part) for part in split_parts(table_x))
    table_zx = jnp.asarray(rounded(table_zx))
    y_parts = jnp.asarray(np.concatenate(split_parts(table_y), axis=0))
    inverse_y = jnp.asarray(rounded(table_y.T))
    weight_z = np.where(np.arange(KZ) == 0, 1.0, 2.0) / (x_cells * y_cells * z_cells)
    scale = jnp.asarray(np.tile(weight_z, ky_local)[None].astype(np.float32))
    mixing = jnp.kron(conv_weight.T, jnp.eye(ROWS, dtype=bf16))
    mode_cells = ky_local * KZ
    groups = 2 * kx_local
    rows = channels * ky_local
    width = groups * KZ
    blocked = groups == ky_local and width % 128 == 0

    def whole(shape):
        return pl.BlockSpec(shape, lambda *x: (0,) * len(shape))

    def cells_at(index, count=1):
        return pl.BlockSpec((count, channels, y_cells, z_cells), lambda x: (index(x), 0, 0, 0))

    def zx_at(index, count=1):
        return pl.BlockSpec((count, 2 * z_cells, lanes), lambda x: (index(x), 0, 0))

    params = pltpu.CompilerParams(
        dimension_semantics=("arbitrary",), vmem_limit_bytes=VMEM_BYTES
    )
    loose = pltpu.CompilerParams(vmem_limit_bytes=VMEM_BYTES)
    coefs_shape = (slabs, rows, lanes)
    coefs_out = jax.ShapeDtypeStruct(coefs_shape, bf16)
    total_shape = (channels * KY, lanes)
    modes_shape = (channels * KY, 2 * z_cells)

    def over(values, axis):
        return lax.all_to_all(values, axis, split_axis=0, concat_axis=0, tiled=True)

    def across_samples(coefs):
        per_step = max(1, 256 // width)
        block = pl.BlockSpec((slabs, lanes, per_step * width), lambda d: (0, 0, d))
        modes = pl.pallas_call(
            to_modes_kernel,
            grid=(data_count // per_step,),
            in_specs=[whole(coefs_shape), block, block],
            out_specs=pl.BlockSpec((per_step, rows, width), lambda d: (d, 0, 0)),
            out_shape=jax.ShapeDtypeStruct((data_count, rows, width), f32),
            compiler_params=params,
        )(over(coefs, "mp"), x_upper, x_lower)
        moved = over(modes, "dp")
        if not blocked:
            moved = moved.reshape(data_count, channels, ky_local, groups, KZ)
            moved = jnp.transpose(moved, (0, 3, 1, 2, 4))
            moved = moved.reshape(data_count, groups, channels, mode_cells)
        return moved

    with jax.named_scope("forward_fields"):
        coefs = pl.pallas_call(
            forward_kernel,
            grid=(slab_len // 4,),
            in_specs=[cells_at(lambda x: x, 4), whole(y_parts.shape), zx_at(lambda x: x, 4)],
            out_specs=whole(coefs_shape),
            out_shape=coefs_out,
            scratch_shapes=[
                pltpu.VMEM((channels * KY, 4 * z_cells), bf16),
                pltpu.VMEM((channels * KY, 4 * z_cells), bf16),
                pltpu.VMEM(total_shape, f32),
            ],
            compiler_params=params,
        )(fields[0], y_parts, table_zx)
    spectra = across_samples(coefs)

    opened_shape = (data_count, groups, channels, mode_cells)
    mixed_shape = (data_count, rows, width) if blocked else opened_shape
    with jax.named_scope("mix_modes"):
        local_mixed, opened = pl.pallas_call(
            functools.partial(mix_kernel, blocked),
            out_shape=[
                jax.ShapeDtypeStruct(mixed_shape, bf16),
                jax.ShapeDtypeStruct(opened_shape, f32),
            ],
            scratch_shapes=[pltpu.VMEM((rows, width), f32)],
            compiler_params=loose,
        )(spectra, spectral_weight, scale)
    if not blocked:
        local_mixed = local_mixed.reshape(data_count, groups, channels, ky_local, KZ)
        local_mixed = jnp.transpose(local_mixed, (0, 2, 3, 1, 4)).reshape(data_count, rows, width)
    slab_block = pl.BlockSpec((1, lanes, KX * 2 * KZ), lambda m: (m, 0, 0))
    slab_mixed = pl.pallas_call(
        from_modes_kernel,
        grid=(slabs,),
        in_specs=[whole((data_count, rows, width)), slab_block, slab_block],
        out_specs=pl.BlockSpec((1, rows, lanes), lambda m: (m, 0, 0)),
        out_shape=coefs_out,
        compiler_params=params,
    )(over(local_mixed, "dp"), x_upper, x_lower)
    mixed_coefs = over(slab_mixed, "mp")

    with jax.named_scope("slope_and_back"):
        back_coefs = pl.pallas_call(
            slope_kernel,
            grid=(slab_len // 2,),
            in_specs=[
                pl.BlockSpec(memory_space=pltpu.SMEM),
                cells_at(lambda x: 0),
                cells_at(lambda x: 2 * x + 1),
                cells_at(lambda x: jnp.minimum(2 * x + 2, slab_len - 1)),
                cells_at(lambda x: x, 2),
                whole(coefs_shape),
                whole(mixing.shape),
                whole(y_parts.shape),
                whole(inverse_y.shape),
                zx_at(lambda x: jnp.maximum(2 * x - 1, 0)),
                zx_at(lambda x: 2 * x),
                zx_at(lambda x: 2 * x + 1),
                zx_at(lambda x: jnp.minimum(2 * x + 2, slab_len - 1)),
            ],
            out_specs=whole(coefs_shape),
            out_shape=coefs_out,
            scratch_shapes=[pltpu.VMEM(total_shape, bf16)]
            + [pltpu.VMEM(modes_shape, bf16)] * 2
            + [pltpu.VMEM((channels, y_cells, z_cells), f32)] * 2
            + [pltpu.VMEM(modes_shape, bf16)] * 2
            + [pltpu.VMEM(total_shape, f32)],
            compiler_params=params,
        )(
            conv_bias,
            fields[0],
            fields[0],
            fields[0],
            cotangent[0],
            mixed_coefs,
            mixing,
            y_parts,
            inverse_y,
            table_zx,
            table_zx,
            table_zx,
            table_zx,
        )
    back = across_samples(back_coefs)

    with jax.named_scope("weight_gradient"):
        return pl.pallas_call(
            functools.partial(grad_kernel, blocked),
            out_shape=jax.ShapeDtypeStruct(spectral_weight.shape, f32),
            scratch_shapes=[pltpu.VMEM(opened_shape, f32)],
            compiler_params=loose,
        )(opened, back, scale)


def solution(mesh):
    return jax.shard_map(
        shards,
        mesh=mesh,
        in_specs=(
            P("dp", "mp", None, None, None),
            P("dp", "mp", None, None, None),
            P("dp", None, None, None, "mp"),
            P(),
            P(),
        ),
        out_specs=P("dp", None, None, None, "mp"),
        check_vma=False,
    )
```

```python
import functools
import math

import jax
import jax.numpy as jnp
import ml_dtypes
import numpy as np
from jax import lax
from jax.experimental import pallas as pl
from jax.experimental.pallas import tpu as pltpu
from jax.sharding import PartitionSpec as P

KX = 32
KY = 32
KZ = 16
ROWS = 16
VMEM_BYTES = 50 * 2**20

f32 = jnp.float32
bf16 = jnp.bfloat16


def kept_modes(count, length):
    indices = np.arange(count)
    return np.where(indices < count // 2, indices, length - count + indices)


def rounded(values):
    return np.asarray(values, np.float32).astype(ml_dtypes.bfloat16)


def split_parts(values):
    upper = rounded(values)
    return upper, rounded(values - upper.astype(np.float64))


def make_tables(x_cells, y_cells, z_cells, slabs):
    slab_len = x_cells // slabs
    kx = kept_modes(KX, x_cells)
    kx = np.where(kx >= x_cells // 2, kx - x_cells, kx)
    part = np.exp(-2j * math.pi * np.outer(kx, np.arange(slab_len)) / x_cells)
    left, scale, right = np.linalg.svd(part, full_matrices=False)
    rank = int(np.sum(scale > scale[0] * np.finfo(np.float32).eps))
    rank = min(rank + rank % 2, slab_len)
    left = left[:, :rank] * scale[:rank]
    right = right[:rank]
    shifts = np.exp(-2j * math.pi * np.outer(kx, np.arange(slabs) * slab_len) / x_cells)
    outer = shifts[:, :, None] * left[:, None, :]
    table_x = np.zeros((KX, 2, slabs, rank, 2))
    table_x[:, 0, :, :, 0] = outer.real
    table_x[:, 0, :, :, 1] = -outer.imag
    table_x[:, 1, :, :, 0] = outer.imag
    table_x[:, 1, :, :, 1] = outer.real
    table_x = table_x.reshape(KX * 2, slabs, rank * 2)
    table_x = np.stack([np.kron(table_x[:, m].T, np.eye(KZ)) for m in range(slabs)])
    wave_z = np.exp(-2j * math.pi * np.outer(np.arange(z_cells), np.arange(KZ)) / z_cells)
    inner = right.T[:, None, :, None] * wave_z[None, :, None, :]
    table_zx = np.zeros((slab_len, 2, z_cells, rank, 2, KZ))
    table_zx[:, 0, :, :, 0] = inner.real
    table_zx[:, 1, :, :, 0] = -inner.imag
    table_zx[:, 0, :, :, 1] = inner.imag
    table_zx[:, 1, :, :, 1] = inner.real
    table_zx = table_zx.reshape(slab_len, 2 * z_cells, rank * 2 * KZ)
    phase_y = 2.0 * math.pi * np.outer(kept_modes(KY, y_cells), np.arange(y_cells)) / y_cells
    table_y = np.concatenate([np.cos(phase_y), -np.sin(phase_y)], axis=0)
    return rank, table_x, table_zx, table_y


def dot(left, right, contract=((1,), (0,))):
    return lax.dot_general(left, right, (contract, ((), ())), preferred_element_type=f32)


def y_modes(pair, table, modes_ref, channel, z_cells, offset=0):
    both = dot(table, pair)
    half = 2 * KY
    total = both[:half] + both[half:]
    for i in range(2):
        one = total[:, i * z_cells : (i + 1) * z_cells].astype(bf16)
        rows = pl.ds((channel + i) * KY, KY)
        modes_ref[rows, offset : offset + z_cells] = one[:KY]
        modes_ref[rows, offset + z_cells : offset + 2 * z_cells] = one[KY:]


def column_chunks(lanes):
    return [(start, min(start + 256, lanes)) for start in range(0, lanes, 256)]


def store_blocks(total_ref, out_ref, channels):
    blocks, rows, _ = out_ref.shape
    ky_local = rows // channels
    group = max(1, ROWS // ky_local)
    for b in range(blocks):
        for c in range(0, channels, group):
            parts = [
                total_ref[(c + i) * KY + b * ky_local : (c + i) * KY + (b + 1) * ky_local, :]
                for i in range(group)
            ]
            out_ref[b, c * ky_local : (c + group) * ky_local, :] = jnp.concatenate(
                parts, axis=0
            ).astype(bf16)


def forward_kernel(fields_ref, table_y_ref, table_zx_ref, out_ref, first_ref, second_ref, total_ref):
    cells, channels, _, z_cells = fields_ref.shape
    lanes = total_ref.shape[1]
    step = pl.program_id(0)
    table = table_y_ref[...]

    @pl.when(step == 0)
    def _():
        total_ref[...] = jnp.zeros_like(total_ref)

    def inner(modes_ref, cell, start, stop):
        both = table_zx_ref[cell : cell + 2, :, start:stop].reshape(4 * z_cells, stop - start)
        total_ref[:, start:stop] += dot(modes_ref[...], both)

    pending = []
    for half, modes_ref in enumerate((first_ref, second_ref)):
        cell = 2 * half
        for c in range(0, channels, 2):
            for i in range(2):
                pair = jnp.concatenate(
                    [fields_ref[cell + i, c], fields_ref[cell + i, c + 1]], axis=1
                )
                y_modes(pair, table, modes_ref, c, z_cells, 2 * i * z_cells)
            if pending and c % 4 == 2:
                pending.pop(0)()
        for todo in pending:
            todo()
        pending = [
            functools.partial(inner, modes_ref, cell, start, stop)
            for start, stop in column_chunks(lanes)
        ]
    for todo in pending:
        todo()

    @pl.when(step == pl.num_programs(0) - 1)
    def _():
        store_blocks(total_ref, out_ref, channels)


def gelu_slope(values):
    size = jnp.abs(values)
    bell = jnp.exp2(values * values * (-0.5 * math.log2(math.e)))
    t = pl.reciprocal(1.0 + size * (0.3275911 * math.sqrt(0.5)), approx=True)
    tail = t * (
        0.5 * 0.254829592
        + t * (0.5 * -0.284496736 + t * (0.5 * 1.421413741 + t * (0.5 * -1.453152027 + t * (0.5 * 1.061405429))))
    )
    part = bell * (size * 0.3989422804014327 - tail)
    return jnp.where(values >= 0.0, 1.0 + part, -part)


def slope_kernel(
    bias_ref,
    fields_first_ref,
    fields_odd_ref,
    fields_next_ref,
    cotangent_ref,
    mixed_ref,
    conv_ref,
    table_y_ref,
    inverse_y_ref,
    zx_before_ref,
    zx_even_ref,
    zx_last_ref,
    inverse_first_ref,
    inverse_odd_ref,
    inverse_next_ref,
    out_ref,
    rows_ref,
    back_even_ref,
    back_odd_ref,
    pre_even_ref,
    pre_odd_ref,
    modes_even_ref,
    modes_odd_ref,
    total_ref,
):
    _, channels, y_cells, z_cells = cotangent_ref.shape
    lanes = total_ref.shape[1]
    count = channels * KY
    step = pl.program_id(0)
    last = pl.num_programs(0) - 1
    table = table_y_ref[...]
    inverse_y = inverse_y_ref[...]
    mixing = conv_ref[...]

    def ahead(fields_ref, inverse_ref, back_ref, pre_ref):
        def inverse(start, stop):
            back_ref[start:stop, :] = dot(rows_ref[start:stop, :], inverse_ref[0]).astype(bf16)

        def convolve(g):
            pair = jnp.concatenate(
                [
                    fields_ref[0, :, g : g + ROWS, :].reshape(channels * ROWS, z_cells),
                    fields_ref[0, :, g + ROWS : g + 2 * ROWS, :].reshape(channels * ROWS, z_cells),
                ],
                axis=1,
            )
            conv = dot(mixing, pair)
            for i in range(2):
                rows = slice(g + i * ROWS, g + (i + 1) * ROWS)
                pre_ref[:, rows, :] = conv[:, i * z_cells : (i + 1) * z_cells].reshape(
                    channels, ROWS, z_cells
                )

        return [
            functools.partial(inverse, 0, count // 2),
            functools.partial(inverse, count // 2, count),
        ] + [functools.partial(convolve, g) for g in range(0, y_cells, 2 * ROWS)]

    def behind(modes_ref, zx_ref):
        def inner(start, stop):
            total_ref[:, start:stop] += dot(modes_ref[...], zx_ref[0, :, start:stop])

        return [functools.partial(inner, start, stop) for start, stop in column_chunks(lanes)]

    def inverse_pair(back_ref, o):
        columns = []
        for i in range(2):
            one = back_ref[(o + i) * KY : (o + i + 1) * KY, :]
            columns.append(jnp.concatenate([one[:, :z_cells], one[:, z_cells:]], axis=0))
        return dot(inverse_y, jnp.concatenate(columns, axis=1))

    def slope_pair(cell, spectral, pre_ref, o):
        deltas = []
        for i in range(2):
            pre = spectral[:, i * z_cells : (i + 1) * z_cells] + pre_ref[o + i] + bias_ref[o + i]
            deltas.append((cotangent_ref[cell, o + i].astype(f32) * gelu_slope(pre)).astype(bf16))
        return jnp.concatenate(deltas, axis=1)

    @pl.when(step == 0)
    def _():
        blocks = mixed_ref.shape[0]
        per_block = mixed_ref.shape[1]
        ky_local = per_block // channels
        for b in range(blocks):
            total_ref[b * per_block : (b + 1) * per_block, :] = mixed_ref[b].astype(f32)
        for o in range(channels):
            parts = [
                total_ref[b * per_block + o * ky_local : b * per_block + (o + 1) * ky_local, :]
                for b in range(blocks)
            ]
            rows_ref[o * KY : (o + 1) * KY, :] = jnp.concatenate(parts, axis=0).astype(bf16)
        total_ref[...] = jnp.zeros_like(total_ref)
        modes_odd_ref[...] = jnp.zeros_like(modes_odd_ref)
        for todo in ahead(fields_first_ref, inverse_first_ref, back_even_ref, pre_even_ref):
            todo()

    even = (0, back_even_ref, pre_even_ref, modes_even_ref)
    odd = (1, back_odd_ref, pre_odd_ref, modes_odd_ref)
    beside = {
        0: ahead(fields_odd_ref, inverse_odd_ref, back_odd_ref, pre_odd_ref)
        + behind(modes_odd_ref, zx_before_ref),
        1: ahead(fields_next_ref, inverse_next_ref, back_even_ref, pre_even_ref)
        + behind(modes_even_ref, zx_even_ref),
    }
    items = [(own, o) for own in (even, odd) for o in range(0, channels, 2)]
    spectral = inverse_pair(back_even_ref, 0)
    delta = None
    for n, ((cell, _, pre_ref, modes_ref), o) in enumerate(items):
        if beside[cell]:
            beside[cell].pop(0)()
        if o + 2 >= channels:
            while beside[cell]:
                beside[cell].pop(0)()
        following = None
        if n + 1 < len(items):
            (_, back_ref, _, _), later = items[n + 1]
            following = inverse_pair(back_ref, later)
        if n > 0:
            (_, _, _, earlier_ref), earlier = items[n - 1]
            y_modes(delta, table, earlier_ref, earlier, z_cells)
        delta = slope_pair(cell, spectral, pre_ref, o)
        spectral = following
    y_modes(delta, table, modes_odd_ref, channels - 2, z_cells)

    @pl.when(step == last)
    def _():
        for todo in behind(modes_odd_ref, zx_last_ref):
            todo()
        store_blocks(total_ref, out_ref, channels)


def to_modes_kernel(coefs_ref, upper_ref, lower_ref, out_ref):
    total = jnp.zeros((coefs_ref.shape[1], upper_ref.shape[2]), f32)
    for m in range(coefs_ref.shape[0]):
        total += dot(coefs_ref[m], upper_ref[m]) + dot(coefs_ref[m], lower_ref[m])
    width = out_ref.shape[2]
    for i in range(out_ref.shape[0]):
        out_ref[i] = total[:, i * width : (i + 1) * width]


def from_modes_kernel(modes_ref, upper_ref, lower_ref, out_ref):
    modes = jnp.concatenate([modes_ref[i] for i in range(modes_ref.shape[0])], axis=1)
    flip = ((1,), (1,))
    out_ref[0] = (dot(modes, upper_ref[0], flip) + dot(modes, lower_ref[0], flip)).astype(bf16)


def swap_groups(parts):
    lanes = parts[0].shape[1]
    group = lax.broadcasted_iota(jnp.int32, parts[0].shape, 1) // KZ
    results = []
    for j in range(len(parts)):
        total = parts[j]
        for i, part in enumerate(parts):
            if i != j:
                moved = pltpu.roll(part, ((i - j) * KZ) % lanes, 1)
                total = jnp.where(group == i, moved, total)
        results.append(total)
    return results


def open_rows(wire_ref, s, channels):
    ky_local = wire_ref.shape[1] // channels
    return swap_groups(
        [wire_ref[s, pl.ds(k, channels, stride=ky_local), :] for k in range(ky_local)]
    )


def mix_kernel(blocked, spectra_ref, weight_ref, scale_ref, out_ref, opened_ref, rows_ref):
    samples = spectra_ref.shape[0]
    kx_local, _, channels, _, mode_cells = weight_ref.shape
    scale = scale_ref[...]

    def one_sample(s, carry):
        if blocked:
            for g, part in enumerate(open_rows(spectra_ref, s, channels)):
                opened_ref[s, g] = part
        else:
            opened_ref[s] = spectra_ref[s]
        results = []
        for k in range(kx_local):
            real = jnp.zeros((channels, mode_cells), f32)
            imag = jnp.zeros((channels, mode_cells), f32)
            for c in range(channels):
                spec_re = opened_ref[s, 2 * k, c : c + 1, :]
                spec_im = opened_ref[s, 2 * k + 1, c : c + 1, :]
                real_w = weight_ref[k, 0, c].astype(f32)
                imag_w = weight_ref[k, 1, c].astype(f32)
                real += spec_re * real_w - spec_im * imag_w
                imag += spec_re * imag_w + spec_im * real_w
            results += [real * scale, imag * scale]
        if blocked:
            ky_local = rows_ref.shape[0] // channels
            for k, part in enumerate(swap_groups(results)):
                rows_ref[pl.ds(k, channels, stride=ky_local), :] = part
            out_ref[s] = rows_ref[...].astype(bf16)
        else:
            for g, part in enumerate(results):
                out_ref[s, g] = part.astype(bf16)
        return carry

    lax.fori_loop(0, samples, one_sample, 0)


def grad_kernel(blocked, spectra_ref, back_ref, scale_ref, out_ref, opened_ref):
    kx_local, _, channels, _, mode_cells = out_ref.shape
    samples = spectra_ref.shape[0]
    scale = scale_ref[...]
    for s in range(samples):
        if blocked:
            for g, part in enumerate(open_rows(back_ref, s, channels)):
                opened_ref[s, g] = part * scale
        else:
            opened_ref[s] = back_ref[s] * scale

    def one_channel(c, carry):
        for k in range(kx_local):
            real = jnp.zeros((channels, mode_cells), f32)
            imag = jnp.zeros((channels, mode_cells), f32)
            for s in range(samples):
                spec_re = spectra_ref[s, 2 * k, pl.ds(c, 1), :]
                spec_im = spectra_ref[s, 2 * k + 1, pl.ds(c, 1), :]
                back_re = opened_ref[s, 2 * k]
                back_im = opened_ref[s, 2 * k + 1]
                real += spec_re * back_re + spec_im * back_im
                imag += spec_re * back_im - spec_im * back_re
            out_ref[k, 0, c] = real
            out_ref[k, 1, c] = imag
        return carry

    lax.fori_loop(0, channels, one_channel, 0)


def shards(fields, cotangent, spectral_weight, conv_weight, conv_bias):
    _, slab_len, channels, y_cells, z_cells = fields.shape
    slabs = lax.axis_size("mp")
    data_count = lax.axis_size("dp")
    kx_local = spectral_weight.shape[0]
    ky_local = KY // slabs
    x_cells = slab_len * slabs
    rank, table_x, table_zx, table_y = make_tables(x_cells, y_cells, z_cells, slabs)
    lanes = rank * 2 * KZ
    x_upper, x_lower = (jnp.asarray(part) for part in split_parts(table_x))
    inverse_zx = jnp.asarray(rounded(np.swapaxes(table_zx, 1, 2)))
    table_zx = jnp.asarray(rounded(table_zx))
    y_parts = jnp.asarray(np.concatenate(split_parts(table_y), axis=0))
    inverse_y = jnp.asarray(rounded(table_y.T))
    weight_z = np.where(np.arange(KZ) == 0, 1.0, 2.0) / (x_cells * y_cells * z_cells)
    scale = jnp.asarray(np.tile(weight_z, ky_local)[None].astype(np.float32))
    mixing = jnp.kron(conv_weight.T, jnp.eye(ROWS, dtype=bf16))
    mode_cells = ky_local * KZ
    groups = 2 * kx_local
    rows = channels * ky_local
    width = groups * KZ
    blocked = groups == ky_local and width % 128 == 0

    def whole(shape):
        return pl.BlockSpec(shape, lambda *x: (0,) * len(shape))

    def cells_at(index, count=1):
        return pl.BlockSpec((count, channels, y_cells, z_cells), lambda x: (index(x), 0, 0, 0))

    def zx_at(index, count=1):
        return pl.BlockSpec((count, 2 * z_cells, lanes), lambda x: (index(x), 0, 0))

    def inverse_at(index):
        return pl.BlockSpec((1, lanes, 2 * z_cells), lambda x: (index(x), 0, 0))

    params = pltpu.CompilerParams(
        dimension_semantics=("arbitrary",), vmem_limit_bytes=VMEM_BYTES
    )
    loose = pltpu.CompilerParams(vmem_limit_bytes=VMEM_BYTES)
    coefs_shape = (slabs, rows, lanes)
    coefs_out = jax.ShapeDtypeStruct(coefs_shape, bf16)
    total_shape = (channels * KY, lanes)
    modes_shape = (channels * KY, 2 * z_cells)

    def over(values, axis):
        return lax.all_to_all(values, axis, split_axis=0, concat_axis=0, tiled=True)

    def across_samples(coefs):
        per_step = max(1, 256 // width)
        block = pl.BlockSpec((slabs, lanes, per_step * width), lambda d: (0, 0, d))
        modes = pl.pallas_call(
            to_modes_kernel,
            grid=(data_count // per_step,),
            in_specs=[whole(coefs_shape), block, block],
            out_specs=pl.BlockSpec((per_step, rows, width), lambda d: (d, 0, 0)),
            out_shape=jax.ShapeDtypeStruct((data_count, rows, width), f32),
            compiler_params=params,
        )(over(coefs, "mp"), x_upper, x_lower)
        moved = over(modes, "dp")
        if not blocked:
            moved = moved.reshape(data_count, channels, ky_local, groups, KZ)
            moved = jnp.transpose(moved, (0, 3, 1, 2, 4))
            moved = moved.reshape(data_count, groups, channels, mode_cells)
        return moved

    with jax.named_scope("forward_fields"):
        coefs = pl.pallas_call(
            forward_kernel,
            grid=(slab_len // 4,),
            in_specs=[cells_at(lambda x: x, 4), whole(y_parts.shape), zx_at(lambda x: x, 4)],
            out_specs=whole(coefs_shape),
            out_shape=coefs_out,
            scratch_shapes=[
                pltpu.VMEM((channels * KY, 4 * z_cells), bf16),
                pltpu.VMEM((channels * KY, 4 * z_cells), bf16),
                pltpu.VMEM(total_shape, f32),
            ],
            compiler_params=params,
        )(fields[0], y_parts, table_zx)
    spectra = across_samples(coefs)

    opened_shape = (data_count, groups, channels, mode_cells)
    mixed_shape = (data_count, rows, width) if blocked else opened_shape
    with jax.named_scope("mix_modes"):
        local_mixed, opened = pl.pallas_call(
            functools.partial(mix_kernel, blocked),
            out_shape=[
                jax.ShapeDtypeStruct(mixed_shape, bf16),
                jax.ShapeDtypeStruct(opened_shape, f32),
            ],
            scratch_shapes=[pltpu.VMEM((rows, width), f32)],
            compiler_params=loose,
        )(spectra, spectral_weight, scale)
    if not blocked:
        local_mixed = local_mixed.reshape(data_count, groups, channels, ky_local, KZ)
        local_mixed = jnp.transpose(local_mixed, (0, 2, 3, 1, 4)).reshape(data_count, rows, width)
    slab_block = pl.BlockSpec((1, lanes, KX * 2 * KZ), lambda m: (m, 0, 0))
    slab_mixed = pl.pallas_call(
        from_modes_kernel,
        grid=(slabs,),
        in_specs=[whole((data_count, rows, width)), slab_block, slab_block],
        out_specs=pl.BlockSpec((1, rows, lanes), lambda m: (m, 0, 0)),
        out_shape=coefs_out,
        compiler_params=params,
    )(over(local_mixed, "dp"), x_upper, x_lower)
    mixed_coefs = over(slab_mixed, "mp")

    with jax.named_scope("slope_and_back"):
        back_coefs = pl.pallas_call(
            slope_kernel,
            grid=(slab_len // 2,),
            in_specs=[
                pl.BlockSpec(memory_space=pltpu.SMEM),
                cells_at(lambda x: 0),
                cells_at(lambda x: 2 * x + 1),
                cells_at(lambda x: jnp.minimum(2 * x + 2, slab_len - 1)),
                cells_at(lambda x: x, 2),
                whole(coefs_shape),
                whole(mixing.shape),
                whole(y_parts.shape),
                whole(inverse_y.shape),
                zx_at(lambda x: jnp.maximum(2 * x - 1, 0)),
                zx_at(lambda x: 2 * x),
                zx_at(lambda x: slab_len - 1),
                inverse_at(lambda x: 0),
                inverse_at(lambda x: 2 * x + 1),
                inverse_at(lambda x: jnp.minimum(2 * x + 2, slab_len - 1)),
            ],
            out_specs=whole(coefs_shape),
            out_shape=coefs_out,
            scratch_shapes=[pltpu.VMEM(total_shape, bf16)]
            + [pltpu.VMEM(modes_shape, bf16)] * 2
            + [pltpu.VMEM((channels, y_cells, z_cells), f32)] * 2
            + [pltpu.VMEM(modes_shape, bf16)] * 2
            + [pltpu.VMEM(total_shape, f32)],
            compiler_params=params,
        )(
            conv_bias,
            fields[0],
            fields[0],
            fields[0],
            cotangent[0],
            mixed_coefs,
            mixing,
            y_parts,
            inverse_y,
            table_zx,
            table_zx,
            table_zx,
            inverse_zx,
            inverse_zx,
            inverse_zx,
        )
    back = across_samples(back_coefs)

    with jax.named_scope("weight_gradient"):
        return pl.pallas_call(
            functools.partial(grad_kernel, blocked),
            out_shape=jax.ShapeDtypeStruct(spectral_weight.shape, f32),
            scratch_shapes=[pltpu.VMEM(opened_shape, f32)],
            compiler_params=loose,
        )(opened, back, scale)


def solution(mesh):
    return jax.shard_map(
        shards,
        mesh=mesh,
        in_specs=(
            P("dp", "mp", None, None, None),
            P("dp", "mp", None, None, None),
            P("dp", None, None, None, "mp"),
            P(),
            P(),
        ),
        out_specs=P("dp", None, None, None, "mp"),
        check_vma=False,
    )
```
